32 devices in a mesh: gx: 2 (over core), gy: 4 (over y, x), gz: 4 (over z).
Axes of the slice: x: 2, y: 2, z: 4, core: 2. Of those that a mesh axis runs over, the one named last changes fastest.
Arguments:
- tokens: bfloat16 [512, 8192], P('gy', ('gz', 'gx')), may hold values from -6 to 6
- gate_weight: bfloat16 [8192, 8192], P('gz', ('gx', 'gy')), may hold values from -0.0625 to 0.0625
- up_weight: bfloat16 [8192, 8192], P('gz', ('gx', 'gy')), may hold values from -0.0625 to 0.0625
- down_weight: bfloat16 [8192, 8192], P('gz', ('gx', 'gy')), may hold values from -0.0625 to 0.0625
- out_grad: bfloat16 [512, 8192], P('gy', ('gz', 'gx')), may hold values from -6 to 6
Outputs:
- output: bfloat16 [512, 8192], P('gy', ('gz', 'gx'))
- tokens_grad: bfloat16 [512, 8192], P('gy', ('gz', 'gx'))
- gate_grad_w: float32 [8192, 8192], P('gz', ('gx', 'gy'))
- up_grad_w: float32 [8192, 8192], P('gz', ('gx', 'gy'))
- down_grad_w: float32 [8192, 8192], P('gz', ('gx', 'gy'))
The draws below stay inside these ranges and needn't reach their ends.
All inputs are finite; a program needn't handle non-finite values.
Results may differ from the reference program's by a relative error of at most 0.023.
Values may be sent and summed in bfloat16 or wider, within the bound.
No kernel may reach another device: no remote copies, remote signals or barrier semaphores. Data moves between devices by JAX's collectives and lax.ppermute only.
A program may use at most 192 MiB of HBM per device.

```python
import jax
import jax.numpy as jnp
from jax import lax

D = 8192
FF = 8192
TOKENS = 512
N_GX = 2
N_GZ = 4


def level_of(key, dims, split, smallest, largest):
    factor_of, own = 1.0, jax.random.fold_in(key, 6)
    for axis_at, parts in split:
        heights = jnp.exp(jax.random.uniform(jax.random.fold_in(own, axis_at), (parts,), jnp.float32, smallest / len(split), largest / len(split)))
        factor_of = factor_of * jnp.repeat(heights, dims[axis_at] // parts).reshape([-1 if axis == axis_at else 1 for axis in range(len(dims))])
    return factor_of


def normal_values(stream_key, dims, spread, limit, pieces=(), kind=jnp.bfloat16):
    gain = level_of(stream_key, dims, pieces, -0.22, 0.18) if pieces else 1.0
    array = jax.random.normal(stream_key, dims, jnp.float32) * spread * gain
    return jnp.minimum(jnp.maximum(array, -limit), limit).astype(kind)


def setup_inputs(seed: int = 0) -> dict:
    seeds = jax.random.split(jax.random.key(seed), 6)
    tokens = normal_values(seeds[0], (TOKENS, D), 1.0, 6.0, ((0, 4), (1, 8)))
    gate_weight = normal_values(seeds[1], (D, FF), D ** -0.5, 0.0625, ((0, 4), (1, 8)))
    up_weight = normal_values(seeds[2], (D, FF), D ** -0.5, 0.0625, ((0, 4), (1, 8)))
    down_weight = normal_values(seeds[3], (D, FF), FF ** -0.5, 0.0625, ((0, 4), (1, 8)))
    out_grad = normal_values(seeds[4], (TOKENS, D), 1.0, 6.0, ((0, 4), (1, 8)))
    return dict(tokens=tokens, gate_weight=gate_weight, up_weight=up_weight, down_weight=down_weight, out_grad=out_grad)


def rounded(value):
    return lax.optimization_barrier(value.astype(jnp.bfloat16)).astype(jnp.float32)


def dot_last(left, right):
    return lax.dot_general(left, right, (((1,), (1,)), ((), ())), preferred_element_type=jnp.float32)


def reference(tokens, gate_weight, up_weight, down_weight, out_grad):
    feat_block = D // N_GZ
    unit_block = FF // N_GX
    gate_value = jnp.zeros((TOKENS, FF), jnp.float32)
    up_value = jnp.zeros((TOKENS, FF), jnp.float32)
    hidden_grad = jnp.zeros((TOKENS, FF), jnp.float32)
    for block_index in range(N_GZ):
        low = block_index * feat_block
        x_part = tokens[:, low:low + feat_block]
        gate_value = gate_value + rounded(jnp.dot(x_part, gate_weight[low:low + feat_block], preferred_element_type=jnp.float32))
        up_value = up_value + rounded(jnp.dot(x_part, up_weight[low:low + feat_block], preferred_element_type=jnp.float32))
        grad_part = out_grad[:, low:low + feat_block]
        hidden_grad = hidden_grad + rounded(jnp.dot(grad_part, down_weight[low:low + feat_block], preferred_element_type=jnp.float32))
    activated = jax.nn.silu(gate_value)
    hidden = (activated * up_value).astype(jnp.bfloat16)
    sigmoid_gate = jax.nn.sigmoid(gate_value)
    gate_grad = (hidden_grad * up_value * sigmoid_gate * (1.0 + gate_value * (1.0 - sigmoid_gate))).astype(jnp.bfloat16)
    up_grad = (hidden_grad * activated).astype(jnp.bfloat16)
    out_sum = jnp.zeros((TOKENS, D), jnp.float32)
    in_sum = jnp.zeros((TOKENS, D), jnp.float32)
    for block_index in range(N_GX):
        low = block_index * unit_block
        high = low + unit_block
        out_sum = out_sum + rounded(dot_last(hidden[:, low:high], down_weight[:, low:high]))
        term = dot_last(gate_grad[:, low:high], gate_weight[:, low:high]) + dot_last(up_grad[:, low:high], up_weight[:, low:high])
        in_sum = in_sum + rounded(term)
    output = out_sum.astype(jnp.bfloat16)
    tokens_grad = in_sum.astype(jnp.bfloat16)
    gate_grad_w = jnp.dot(tokens.T, gate_grad, preferred_element_type=jnp.float32)
    up_grad_w = jnp.dot(tokens.T, up_grad, preferred_element_type=jnp.float32)
    down_grad_w = jnp.dot(out_grad.T, hidden, preferred_element_type=jnp.float32)
    return (output, tokens_grad, gate_grad_w, up_grad_w, down_grad_w)
```

```python
import jax
import jax.numpy as jnp
from jax import lax
from jax.sharding import PartitionSpec as P


def dot(left, right):
    return jnp.dot(left, right, preferred_element_type=jnp.float32)


def dot_last(left, right):
    return lax.dot_general(
        left, right, (((1,), (1,)), ((), ())), preferred_element_type=jnp.float32
    )


def dot_first(left, right):
    return lax.dot_general(
        left, right, (((0,), (0,)), ((), ())), preferred_element_type=jnp.float32
    )


def gather_rows(block):
    rows = lax.all_gather(block, "gy", axis=0, tiled=True)
    return lax.all_gather(rows, "gx", axis=1, tiled=True)


def sum_over_units(part):
    part = lax.psum_scatter(part, "gx", scatter_dimension=1, tiled=True)
    return lax.psum_scatter(part, "gy", scatter_dimension=0, tiled=True)


def per_device(tokens, gate_weight, up_weight, down_weight, out_grad):
    bf16 = jnp.bfloat16
    x_all = gather_rows(tokens)
    g_all = gather_rows(out_grad)
    width = gate_weight.shape[1]
    gate_up = jnp.concatenate(
        [dot(x_all, gate_weight).astype(bf16), dot(x_all, up_weight).astype(bf16)], axis=1
    )
    gate_up = lax.psum_scatter(gate_up, "gz", scatter_dimension=0, tiled=True).astype(jnp.float32)
    hidden_grad = lax.psum_scatter(
        dot(g_all, down_weight).astype(bf16), "gz", scatter_dimension=0, tiled=True
    ).astype(jnp.float32)
    gate_value = gate_up[:, :width]
    up_value = gate_up[:, width:]
    sigmoid_gate = jax.nn.sigmoid(gate_value)
    activated = gate_value * sigmoid_gate
    hidden = (activated * up_value).astype(bf16)
    gate_grad = (
        hidden_grad * up_value * sigmoid_gate * (1.0 + gate_value * (1.0 - sigmoid_gate))
    ).astype(bf16)
    up_grad = (hidden_grad * activated).astype(bf16)
    hidden_all = lax.all_gather(hidden, "gz", axis=0, tiled=True)
    output = sum_over_units(dot_last(hidden_all, down_weight).astype(bf16))
    gate_all = lax.all_gather(gate_grad, "gz", axis=0, tiled=True)
    up_all = lax.all_gather(up_grad, "gz", axis=0, tiled=True)
    tokens_grad = sum_over_units(
        (dot_last(gate_all, gate_weight) + dot_last(up_all, up_weight)).astype(bf16)
    )
    down_grad_w = dot_first(g_all, hidden_all)
    gate_grad_w = dot_first(x_all, gate_all)
    up_grad_w = dot_first(x_all, up_all)
    return (output, tokens_grad, gate_grad_w, up_grad_w, down_grad_w)


def solution(mesh):
    return jax.shard_map(
        per_device,
        mesh=mesh,
        in_specs=(
            P("gy", ("gz", "gx")),
            P("gz", ("gx", "gy")),
            P("gz", ("gx", "gy")),
            P("gz", ("gx", "gy")),
            P("gy", ("gz", "gx")),
        ),
        out_specs=(
            P("gy", ("gz", "gx")),
            P("gy", ("gz", "gx")),
            P("gz", ("gx", "gy")),
            P("gz", ("gx", "gy")),
            P("gz", ("gx", "gy")),
        ),
        check_vma=False,
    )
```

```python
import functools

import jax
import jax.numpy as jnp
from jax import lax
from jax.experimental import pallas as pl
from jax.experimental.pallas import tpu as pltpu
from jax.sharding import PartitionSpec as P

BF16 = jnp.bfloat16
F32 = jnp.float32
MIB = 1 << 20


def after(value, *earlier):
    return lax.optimization_barrier((value, *earlier))[0]


def swap(value, axis, size, mask):
    return lax.ppermute(value, axis, [(i, i ^ mask) for i in range(size)])


def reversed_bits(index, size):
    bits = size.bit_length() - 1
    out = jnp.zeros((), jnp.int32)
    for bit in range(bits):
        out = out | (((index >> bit) & 1) << (bits - 1 - bit))
    return out


def params(limit=40):
    return pltpu.CompilerParams(vmem_limit_bytes=limit * MIB)


def whole(array):
    zeros = (0,) * array.ndim
    return pl.BlockSpec(array.shape, lambda *_: zeros)


def ordered_rows(tokens, out_grad, flip, pieces):
    rows, width = tokens.shape
    piece = rows // pieces

    def kernel(flip_ref, a_ref, b_ref, o_ref):
        o_ref[0] = a_ref[...]
        o_ref[1] = b_ref[...]

    source = pl.BlockSpec((piece, width), lambda i, flip: (i ^ flip[0], 0))
    return pl.pallas_call(
        kernel,
        grid_spec=pltpu.PrefetchScalarGridSpec(
            num_scalar_prefetch=1,
            grid=(pieces,),
            in_specs=[source, source],
            out_specs=pl.BlockSpec((2, piece, width), lambda i, flip: (0, i, 0)),
        ),
        out_shape=jax.ShapeDtypeStruct((2, rows, width), BF16),
        compiler_params=params(),
        name="ordered_rows",
    )(flip, tokens, out_grad)


def forward_products(core, own, other, gate_weight, up_weight, down_weight):
    _, rows, width = own.shape
    depth, units = gate_weight.shape
    tile = min(256, units)
    half = rows // 2

    def kernel(core_ref, own_ref, other_ref, gate_ref, up_ref, down_ref, keep_ref, send_ref):
        here = pl.ds(pl.multiple_of(core_ref[0] * width, width), width)
        there = pl.ds(pl.multiple_of((1 - core_ref[0]) * width, width), width)
        for index, (which, weight) in enumerate(((0, gate_ref), (0, up_ref), (1, down_ref))):
            part = jnp.dot(own_ref[which], weight[here, :], preferred_element_type=F32)
            part += jnp.dot(other_ref[which], weight[there, :], preferred_element_type=F32)
            part = part.astype(BF16)
            keep_ref[index] = part[:half]
            send_ref[index] = part[half:]

    weight = pl.BlockSpec((depth, tile), lambda j, core: (0, j))
    result = pl.BlockSpec((3, half, tile), lambda j, core: (0, 0, j))
    return pl.pallas_call(
        kernel,
        grid_spec=pltpu.PrefetchScalarGridSpec(
            num_scalar_prefetch=1,
            grid=(units // tile,),
            in_specs=[whole(own), whole(other), weight, weight, weight],
            out_specs=[result, result],
        ),
        out_shape=[jax.ShapeDtypeStruct((3, half, units), BF16)] * 2,
        compiler_params=params(),
        name="forward_products",
    )(core, own, other, gate_weight, up_weight, down_weight)


def add_halves(held, received):
    rows = held.shape[1]
    half = rows // 2

    def kernel(a_ref, b_ref, keep_ref, send_ref):
        for index in range(3):
            total = (a_ref[index].astype(F32) + b_ref[index].astype(F32)).astype(BF16)
            keep_ref[index] = total[:half]
            send_ref[index] = total[half:]

    shape = jax.ShapeDtypeStruct((3, half, held.shape[2]), BF16)
    return pl.pallas_call(
        kernel, out_shape=[shape, shape], compiler_params=params(), name="add_halves"
    )(held, received)


def activations(held, received):
    def kernel(a_ref, b_ref, o_ref):
        gate, up, grad = [a_ref[i].astype(F32) + b_ref[i].astype(F32) for i in range(3)]
        sigmoid = jax.nn.sigmoid(gate)
        active = gate * sigmoid
        o_ref[0] = (active * up).astype(BF16)
        o_ref[1] = (grad * up * sigmoid * (1.0 + gate * (1.0 - sigmoid))).astype(BF16)
        o_ref[2] = (grad * active).astype(BF16)

    return pl.pallas_call(
        kernel,
        out_shape=jax.ShapeDtypeStruct(held.shape, BF16),
        compiler_params=params(),
        name="activations",
    )(held, received)


NT = (((1,), (1,)), ((), ()))
TN = (((0,), (0,)), ((), ()))


def backward_products(core, acts, gate_weight, up_weight, down_weight):
    rows = sum(a.shape[1] for a in acts)
    depth, units = gate_weight.shape
    width = depth // 2
    tile = min(256, width)
    steps = width // tile
    count = len(acts)

    def kernel(core_ref, *refs):
        act_refs = refs[:count]
        gate_ref, up_ref, down_ref, keep_ref, send_ref = refs[count:]
        hidden, gate, up = [
            jnp.concatenate([ref[i] for ref in act_refs], axis=0) for i in range(3)
        ]
        out = lax.dot_general(hidden, down_ref[...], NT, preferred_element_type=F32)
        grad = lax.dot_general(gate, gate_ref[...], NT, preferred_element_type=F32)
        grad += lax.dot_general(up, up_ref[...], NT, preferred_element_type=F32)

        @pl.when(pl.program_id(0) < steps)
        def _():
            send_ref[0] = out.astype(BF16)
            send_ref[1] = grad.astype(BF16)

        @pl.when(pl.program_id(0) >= steps)
        def _():
            keep_ref[0] = out.astype(BF16)
            keep_ref[1] = grad.astype(BF16)

    def place(j, core):
        side = jnp.where(j < steps, 1 - core[0], core[0])
        return (side * steps + j % steps, 0)

    weight = pl.BlockSpec((tile, units), place)
    return pl.pallas_call(
        kernel,
        grid_spec=pltpu.PrefetchScalarGridSpec(
            num_scalar_prefetch=1,
            grid=(2 * steps,),
            in_specs=[whole(a) for a in acts] + [weight, weight, weight],
            out_specs=[
                pl.BlockSpec((2, rows, tile), lambda j, core: (0, 0, jnp.maximum(j - steps, 0))),
                pl.BlockSpec((2, rows, tile), lambda j, core: (0, 0, jnp.minimum(j, steps - 1))),
            ],
        ),
        out_shape=[jax.ShapeDtypeStruct((2, rows, width), BF16)] * 2,
        compiler_params=params(),
        name="backward_products",
    )(core, *acts, gate_weight, up_weight, down_weight)


def weight_grads(core, owns, others, acts):
    count = len(owns)
    _, rows, width = owns[0].shape
    units = acts[0][0].shape[2]
    tile = min(256, width)
    steps = width // tile
    flat = [piece for block in acts for piece in block]
    pieces = len(flat)
    total = rows * count

    def kernel(core_ref, *refs):
        own_refs, other_refs = refs[:count], refs[count : 2 * count]
        act_refs = refs[2 * count : 2 * count + pieces]
        gate_out, up_out, down_out, all_acts, left = refs[2 * count + pieces :]
        step = pl.program_id(0)

        @pl.when(step == 0)
        def _():
            low = 0
            for ref in act_refs:
                all_acts[:, low : low + ref.shape[1]] = ref[...]
                low += ref.shape[1]

        columns = pl.ds(pl.multiple_of((step % steps) * tile, tile), tile)

        @pl.when(step < steps)
        def _():
            for index, ref in enumerate(own_refs):
                left[:, index * rows : (index + 1) * rows] = ref[:, :, columns]

        @pl.when(step >= steps)
        def _():
            for index, ref in enumerate(other_refs):
                left[:, index * rows : (index + 1) * rows] = ref[:, :, columns]

        tokens, grads = left[0], left[1]
        down_out[...] = lax.dot_general(grads, all_acts[0], TN, preferred_element_type=F32)
        gate_out[...] = lax.dot_general(tokens, all_acts[1], TN, preferred_element_type=F32)
        up_out[...] = lax.dot_general(tokens, all_acts[2], TN, preferred_element_type=F32)

    def place(j, core):
        side = jnp.where(j < steps, core[0], 1 - core[0])
        return (side * steps + j % steps, 0)

    return pl.pallas_call(
        kernel,
        grid_spec=pltpu.PrefetchScalarGridSpec(
            num_scalar_prefetch=1,
            grid=(2 * steps,),
            in_specs=[whole(a) for a in (*owns, *others, *flat)],
            out_specs=[pl.BlockSpec((tile, units), place)] * 3,
            scratch_shapes=[
                pltpu.VMEM((3, total, units), BF16),
                pltpu.VMEM((2, total, tile), BF16),
            ],
        ),
        out_shape=[jax.ShapeDtypeStruct((2 * width, units), F32)] * 3,
        compiler_params=params(56),
        name="weight_grads",
    )(core, *owns, *others, *flat)


def add_pair(a, b):
    return (a.astype(F32) + b.astype(F32)).astype(BF16)


def final_sum(parts, flip, pieces):
    _, rows, width = parts[0].shape
    piece = rows // pieces
    count = len(parts)

    def kernel(flip_ref, *refs):
        for index, out_ref in enumerate(refs[count:]):
            total = refs[0][index].astype(F32)
            for ref in refs[1:count]:
                total += ref[index].astype(F32)
            out_ref[...] = total.astype(BF16)

    source = pl.BlockSpec((2, piece, width), lambda i, flip: (0, i, 0))
    target = pl.BlockSpec((piece, width), lambda i, flip: (i ^ flip[0], 0))
    return pl.pallas_call(
        kernel,
        grid_spec=pltpu.PrefetchScalarGridSpec(
            num_scalar_prefetch=1,
            grid=(pieces,),
            in_specs=[source] * count,
            out_specs=[target, target],
        ),
        out_shape=[jax.ShapeDtypeStruct((rows, width), BF16)] * 2,
        compiler_params=params(),
        name="final_sum",
    )(flip, *parts)


def per_device(sizes, tokens, gate_weight, up_weight, down_weight, out_grad):
    n_gy, n_gz = sizes["gy"], sizes["gz"]
    levels = n_gz.bit_length() - 1
    core = lax.axis_index("gx").astype(jnp.int32).reshape(1)
    flip = reversed_bits(lax.axis_index("gz").astype(jnp.int32), n_gz).reshape(1)
    weights = (gate_weight, up_weight, down_weight)
    swap_core = functools.partial(swap, axis="gx", size=2, mask=1)

    mine = ordered_rows(tokens, out_grad, flip, n_gz)
    owns = [mine] + [swap(mine, "gy", n_gy, d) for d in range(1, n_gy)]
    others = [swap_core(own) for own in owns]

    def chunk(d):
        keep, send = forward_products(core, owns[d], others[d], *weights)
        for level in range(levels - 1):
            got = swap(send, "gz", n_gz, 1 << level)
            got = yield got
            keep, send = add_halves(keep, got)
        got = swap(send, "gz", n_gz, 1 << (levels - 1))
        got = yield got
        acts = [activations(keep, got)]
        for level in reversed(range(levels)):
            held = acts[0] if len(acts) == 1 else jnp.concatenate(acts, axis=1)
            got = swap(held, "gz", n_gz, 1 << level)
            got = yield got
            acts.append(got)
        return acts

    acts = [None] * n_gy
    runs = [chunk(d) for d in range(n_gy)]
    waiting = [next(run) for run in runs]
    live = list(range(n_gy))
    while live:
        for d in list(live):
            try:
                waiting[d] = runs[d].send(waiting[d])
            except StopIteration as stop:
                acts[d] = stop.value
                live.remove(d)

    parts = []
    for d in range(n_gy):
        keep, send = backward_products(core, acts[d], *weights)
        part = add_pair(keep, swap_core(send))
        parts.append(swap(part, "gy", n_gy, d) if d else part)
    output, tokens_grad = final_sum(parts, flip, n_gz)
    gate_grad_w, up_grad_w, down_grad_w = weight_grads(core, owns, others, acts)
    return (output, tokens_grad, gate_grad_w, up_grad_w, down_grad_w)


def solution(mesh):
    return jax.shard_map(
        functools.partial(per_device, dict(mesh.shape)),
        mesh=mesh,
        in_specs=(
            P("gy", ("gz", "gx")),
            P("gz", ("gx", "gy")),
            P("gz", ("gx", "gy")),
            P("gz", ("gx", "gy")),
            P("gy", ("gz", "gx")),
        ),
        out_specs=(
            P("gy", ("gz", "gx")),
            P("gy", ("gz", "gx")),
            P("gz", ("gx", "gy")),
            P("gz", ("gx", "gy")),
            P("gz", ("gx", "gy")),
        ),
        check_vma=False,
    )
```

```python
import functools

import jax
import jax.numpy as jnp
from jax import lax
from jax.experimental import pallas as pl
from jax.experimental.pallas import tpu as pltpu
from jax.sharding import PartitionSpec as P

BF16 = jnp.bfloat16
F32 = jnp.float32
MIB = 1 << 20
NT = (((1,), (1,)), ((), ()))
TN = (((0,), (0,)), ((), ()))
LOCAL = pl.BlockSpec(memory_space=pltpu.VMEM)
SCALAR = pl.BlockSpec(memory_space=pltpu.SMEM)
ANY = pl.BlockSpec(memory_space=pl.ANY)


def shaped(*dims, dtype=BF16):
    return jax.ShapeDtypeStruct(dims, dtype)


class Line:
    def __init__(self):
        self.last = None

    def call(self, name, kernel, operands, in_specs, out_specs, out_shape, limit=16, **rest):
        if self.last is not None:
            count, inner = len(operands), kernel
            operands, in_specs = [*operands, self.last], [*in_specs, ANY]

            def kernel(*refs):
                inner(*refs[:count], *refs[count + 1 :])

        result = pl.pallas_call(
            kernel,
            in_specs=in_specs,
            out_specs=out_specs,
            out_shape=out_shape,
            compiler_params=pltpu.CompilerParams(vmem_limit_bytes=limit * MIB),
            cost_estimate=pl.CostEstimate(flops=1000, bytes_accessed=1000, transcendentals=0),
            name=name,
            **rest,
        )(*operands)
        self.last = result[0] if isinstance(result, (list, tuple)) else result
        return result


def swap(value, axis, size, mask):
    return lax.ppermute(value, axis, [(i, i ^ mask) for i in range(size)])


def ordered_rows(line, tokens, out_grad, flip, pieces):
    rows, width = tokens.shape
    piece = rows // pieces

    def kernel(flip_ref, a_ref, b_ref, o_ref, sems):
        copies = []
        for index, ref in enumerate((a_ref, b_ref)):
            for at in range(pieces):
                source = pl.ds(pl.multiple_of((at ^ flip_ref[0]) * piece, piece), piece)
                target = o_ref.at[index, at * piece : (at + 1) * piece]
                copies.append(
                    pltpu.make_async_copy(ref.at[source], target, sems.at[index * pieces + at])
                )
        for copy in copies:
            copy.start()
        for copy in copies:
            copy.wait()

    return line.call(
        "ordered_rows",
        kernel,
        [flip, tokens, out_grad],
        [SCALAR, ANY, ANY],
        LOCAL,
        shaped(2, rows, width),
        limit=52,
        scratch_shapes=[pltpu.SemaphoreType.DMA((2 * pieces,))],
    )


def pass_on(line, value):
    def kernel(a_ref, o_ref):
        pass

    return line.call(
        "pass_on",
        kernel,
        [value],
        [ANY],
        ANY,
        shaped(*value.shape),
        limit=1,
        input_output_aliases={0: 0},
    )


def forward_products(line, core, own, other, low, rows, piece, weights):
    width = own.shape[2]
    units = weights[0].shape[1]
    tile = min(256, units)

    def kernel(core_ref, own_ref, other_ref, gate_ref, up_ref, down_ref, last_ref, first_ref):
        here = pl.ds(pl.multiple_of(core_ref[0] * width, width), width)
        there = pl.ds(pl.multiple_of((1 - core_ref[0]) * width, width), width)

        @pl.loop(0, units // tile)
        def _(step):
            columns = pl.ds(pl.multiple_of(step * tile, tile), tile)
            for index, (which, weight) in enumerate(((0, gate_ref), (0, up_ref), (1, down_ref))):
                left = own_ref[which, low : low + rows]
                part = jnp.dot(left, weight[here, columns], preferred_element_type=F32)
                left = other_ref[which, low : low + rows]
                part += jnp.dot(left, weight[there, columns], preferred_element_type=F32)
                part = part.astype(BF16)
                for at in range(0, rows // piece, 2):
                    to = slice(at // 2 * piece, (at // 2 + 1) * piece)
                    last_ref[index, to, columns] = part[at * piece : (at + 1) * piece]
                    first_ref[index, to, columns] = part[(at + 1) * piece : (at + 2) * piece]

    return line.call(
        "forward_products",
        kernel,
        [core, own, other, *weights],
        [SCALAR] + [LOCAL] * 5,
        [LOCAL] * 2,
        [shaped(3, rows // 2, units)] * 2,
    )


def add_on(line, held, received):
    def kernel(a_ref, b_ref, o_ref):
        o_ref[...] = (a_ref[...].astype(F32) + b_ref[...].astype(F32)).astype(BF16)

    return line.call(
        "add_on", kernel, [held, received], [LOCAL] * 2, LOCAL, shaped(*held.shape), limit=4
    )


def activations(line, held, received):
    def kernel(a_ref, b_ref, o_ref):
        gate, up, grad = [a_ref[i].astype(F32) + b_ref[i].astype(F32) for i in range(3)]
        sigmoid = jax.nn.sigmoid(gate)
        active = gate * sigmoid
        o_ref[0] = (active * up).astype(BF16)
        o_ref[1] = (grad * up * sigmoid * (1.0 + gate * (1.0 - sigmoid))).astype(BF16)
        o_ref[2] = (grad * active).astype(BF16)

    return line.call(
        "activations", kernel, [held, received], [LOCAL] * 2, LOCAL, shaped(*held.shape), limit=4
    )


def backward_products(line, core, place, passed, piece, weights):
    count = len(passed)
    _, half, units = passed[0].shape
    rows = 2 * half
    width = weights[0].shape[0] // 2

    def kernel(core_ref, place_ref, *refs):
        passed_refs = refs[:count]
        gate_ref, up_ref, down_ref, keep_ref, send_ref, acts_ref = refs[count:]
        near = jnp.minimum(place_ref[0], count - 1 - place_ref[0])
        for index, ref in enumerate(passed_refs):
            far = index >= count // 2

            @pl.when(near == (count - 1 - index if far else index))
            def _(ref=ref, far=far):
                for at in range(half // piece):
                    to = (2 * at + far) * piece
                    acts_ref[:, to : to + piece] = ref[:, at * piece : (at + 1) * piece]

        def fill(target, side):
            lines = pl.ds(pl.multiple_of(side * width, width), width)
            out = lax.dot_general(down_ref[lines], acts_ref[0], NT, preferred_element_type=F32)
            grad = lax.dot_general(gate_ref[lines], acts_ref[1], NT, preferred_element_type=F32)
            grad += lax.dot_general(up_ref[lines], acts_ref[2], NT, preferred_element_type=F32)
            target[0] = out.astype(BF16).T
            target[1] = grad.astype(BF16).T

        fill(send_ref, 1 - core_ref[0])
        fill(keep_ref, core_ref[0])

    return line.call(
        "backward_products",
        kernel,
        [core, place, *passed, *weights],
        [SCALAR] * 2 + [LOCAL] * (count + 3),
        [LOCAL] * 3,
        [shaped(2, rows, width)] * 2 + [shaped(3, rows, units)],
    )


def weight_grads(line, core, owns, others, acts, spans):
    count, chunks = len(owns), len(acts)
    _, rows, width = owns[0].shape
    units = acts[0].shape[2]
    tile = min(256, width)
    steps = width // tile
    total = rows * count

    def kernel(core_ref, *refs):
        own_refs, other_refs = refs[:count], refs[count : 2 * count]
        act_refs = refs[2 * count : 2 * count + chunks]
        _, gate_out, up_out, down_out, all_acts, left, held, sems = refs[2 * count + chunks :]
        for ref, (low, high) in zip(act_refs, spans):
            all_acts[:, low:high] = ref[...]

        def copies(step, slot):
            side = jnp.where(step < steps, core_ref[0], 1 - core_ref[0])
            line_at = pl.multiple_of((side * steps + lax.rem(step, steps)) * tile, tile)
            return [
                pltpu.make_async_copy(
                    held.at[slot, index], out.at[pl.ds(line_at, tile)], sems.at[slot, index]
                )
                for index, out in enumerate((gate_out, up_out, down_out))
            ]

        @pl.loop(0, 2 * steps)
        def _(step):
            slot = lax.rem(step, 2)
            columns = pl.ds(pl.multiple_of(lax.rem(step, steps) * tile, tile), tile)

            @pl.when(step < steps)
            def _():
                for index, ref in enumerate(own_refs):
                    left[:, index * rows : (index + 1) * rows] = ref[:, :, columns]

            @pl.when(step >= steps)
            def _():
                for index, ref in enumerate(other_refs):
                    left[:, index * rows : (index + 1) * rows] = ref[:, :, columns]

            @pl.when(step >= 2)
            def _():
                for copy in copies(step - 2, slot):
                    copy.wait()

            for index, (which, act) in enumerate(((0, 1), (0, 2), (1, 0))):
                held[slot, index] = lax.dot_general(
                    left[which], all_acts[act], TN, preferred_element_type=F32
                )
            for copy in copies(step, slot):
                copy.start()

        for step in (2 * steps - 2, 2 * steps - 1):
            for copy in copies(step, step % 2):
                copy.wait()

    return line.call(
        "weight_grads",
        kernel,
        [core, *owns, *others, *acts],
        [SCALAR] + [LOCAL] * (2 * count + chunks),
        [ANY] * 4,
        [shaped(16, 128)] + [shaped(2 * width, units, dtype=F32)] * 3,
        limit=24,
        scratch_shapes=[
            pltpu.VMEM((3, total, units), BF16),
            pltpu.VMEM((2, total, tile), BF16),
            pltpu.VMEM((2, 3, tile, units), F32),
            pltpu.SemaphoreType.DMA((2, 3)),
        ],
    )


def final_sum(line, parts, flip, piece):
    rows = sum(part.shape[1] for part in parts[0])
    width = parts[0][0].shape[2]
    flat = [part for block in parts for part in block]

    def kernel(flip_ref, *refs):
        outs = refs[len(flat) :]
        at = 0
        sources = []
        for block in parts:
            spans = []
            for part in block:
                for low in range(0, part.shape[1], piece):
                    spans.append((refs[at], low))
                at += 1
            sources.append(spans)
        for place in range(rows // piece):
            to = pl.ds(pl.multiple_of((place ^ flip_ref[0]) * piece, piece), piece)
            for index, out_ref in enumerate(outs):
                total = 0.0
                for spans in sources:
                    ref, low = spans[place]
                    total += ref[index, low : low + piece].astype(F32)
                out_ref[to] = total.astype(BF16)

    return line.call(
        "final_sum",
        kernel,
        [flip, *flat],
        [SCALAR] + [LOCAL] * len(flat),
        [LOCAL] * 2,
        [shaped(rows, width)] * 2,
    )


WEIGHTS = -1
FOUR = (2, 1, 2, 0, 1, 3, 2, 3, 1, 2, 3, 1, 2, 0, 3, 1, 2, 0, 3, 1, 2, 0, 3, 1, 2, 0, 3, 1, 2, 0, 3, 1, 2, 0, 3, WEIGHTS, 1, 0, 3)


def plan_of(n_gy, n_gz, pieces):
    chunks = [(d, 0, pieces) for d in range(n_gy)]
    if (n_gy, n_gz) == (4, 4):
        return chunks, FOUR
    events = []
    for at, (d, _, _) in enumerate(chunks):
        for k in range(-1 if d else 0, 2 * n_gz + (1 if d else 0)):
            events.append((at + 2 * k, at))
    return chunks, [at for _, at in sorted(events)] + [WEIGHTS]


def per_device(sizes, tokens, gate_weight, up_weight, down_weight, out_grad):
    n_gy, n_gz = sizes["gy"], sizes["gz"]
    pieces = 4
    piece = tokens.shape[0] // pieces
    core = lax.axis_index("gx").astype(jnp.int32).reshape(1)
    level = lax.axis_index("gz").astype(jnp.int32)
    place = level.reshape(1)
    flip = (level >= n_gz // 2).astype(jnp.int32).reshape(1)
    swap_core = functools.partial(swap, axis="gx", size=2, mask=1)
    line = Line()

    def hop(value, step):
        pairs = [(step, step + 1), (n_gz - 1 - step, n_gz - 2 - step)]
        return lax.ppermute(value, "gz", pairs)

    mine = ordered_rows(line, tokens, out_grad, flip, pieces)
    others = [swap_core(mine)] + [None] * (n_gy - 1)
    owns = {0: mine}

    def send_blocks(d):
        step = 1 << d.bit_length()
        while step < n_gy:
            owns[d | step] = swap(owns[d], "gy", n_gy, step)
            step <<= 1

    send_blocks(0)
    weights = (gate_weight, up_weight, down_weight)
    acts = {}

    def chunk(at, d, first_piece, count):
        if others[d] is None:
            yield
            owns[d] = pass_on(line, owns[d])
            others[d] = swap_core(owns[d])
            send_blocks(d)
        yield
        last, first = forward_products(
            line, core, owns[d], others[d], first_piece * piece, count * piece, piece, weights
        )
        value = first
        for step in range(n_gz - 1):
            got = hop(value, step)
            yield
            if step < n_gz - 2:
                value = add_on(line, first if step + 1 < n_gz // 2 else last, got)
        value = activations(line, last, got)
        passed = [value]
        for step in range(n_gz - 1):
            value = hop(value, step)
            yield
            if step < n_gz - 2:
                value = pass_on(line, value)
            passed.append(value)
        keep, send, acts[at] = backward_products(line, core, place, passed, piece, weights)
        got = swap_core(send)
        yield
        part = add_on(line, keep, got)
        if d:
            part = swap(part, "gy", n_gy, d)
            yield
            part = pass_on(line, part)
        parts[d].append(part)
        yield

    plan, order = plan_of(n_gy, n_gz, pieces)
    spans = []
    for d, first_piece, count in plan:
        low = (d * pieces + first_piece) * piece
        spans.append((low, low + count * piece))
    parts = [[] for _ in range(n_gy)]
    runs = [chunk(at, *entry) for at, entry in enumerate(plan)]
    for run in runs:
        next(run)
    for at in order:
        if at == WEIGHTS:
            every = [acts[i] for i in range(len(plan))]
            grads = weight_grads(
                line, core, [owns[d] for d in range(n_gy)], others, every, spans
            )
        else:
            next(runs[at])
    output, tokens_grad = final_sum(line, parts, flip, piece)
    _, gate_grad_w, up_grad_w, down_grad_w = grads
    return (output, tokens_grad, gate_grad_w, up_grad_w, down_grad_w)


def solution(mesh):
    return jax.shard_map(
        functools.partial(per_device, dict(mesh.shape)),
        mesh=mesh,
        in_specs=(
            P("gy", ("gz", "gx")),
            P("gz", ("gx", "gy")),
            P("gz", ("gx", "gy")),
            P("gz", ("gx", "gy")),
            P("gy", ("gz", "gx")),
        ),
        out_specs=(
            P("gy", ("gz", "gx")),
            P("gy", ("gz", "gx")),
            P("gz", ("gx", "gy")),
            P("gz", ("gx", "gy")),
            P("gz", ("gx", "gy")),
        ),
        check_vma=False,
    )
```

```python
import functools

import jax
import jax.numpy as jnp
from jax import lax
from jax.experimental import pallas as pl
from jax.experimental.pallas import tpu as pltpu
from jax.sharding import PartitionSpec as P

BF16 = jnp.bfloat16
F32 = jnp.float32
MIB = 1 << 20
NT = (((1,), (1,)), ((), ()))
TN = (((0,), (0,)), ((), ()))
LOCAL = pl.BlockSpec(memory_space=pltpu.VMEM)
SCALAR = pl.BlockSpec(memory_space=pltpu.SMEM)
ANY = pl.BlockSpec(memory_space=pl.ANY)


def shaped(*dims, dtype=BF16):
    return jax.ShapeDtypeStruct(dims, dtype)


class Line:
    def __init__(self):
        self.last = None

    def call(self, name, kernel, operands, in_specs, out_specs, out_shape, limit=16, cost=1000, **rest):
        if self.last is not None:
            count, inner = len(operands), kernel
            operands, in_specs = [*operands, self.last], [*in_specs, ANY]

            def kernel(*refs):
                inner(*refs[:count], *refs[count + 1 :])

        result = pl.pallas_call(
            kernel,
            in_specs=in_specs,
            out_specs=out_specs,
            out_shape=out_shape,
            compiler_params=pltpu.CompilerParams(vmem_limit_bytes=limit * MIB),
            cost_estimate=pl.CostEstimate(flops=1000, bytes_accessed=cost, transcendentals=0),
            name=name,
            **rest,
        )(*operands)
        self.last = result[0] if isinstance(result, (list, tuple)) else result
        return result


def swap(value, axis, size, mask):
    return lax.ppermute(value, axis, [(i, i ^ mask) for i in range(size)])


def ordered_rows(line, tokens, out_grad, flip, pieces):
    rows, width = tokens.shape
    piece = rows // pieces

    def kernel(flip_ref, a_ref, b_ref, o_ref, sems):
        copies = []
        for index, ref in enumerate((a_ref, b_ref)):
            for at in range(pieces):
                source = pl.ds(pl.multiple_of((at ^ flip_ref[0]) * piece, piece), piece)
                target = o_ref.at[index, at * piece : (at + 1) * piece]
                copies.append(
                    pltpu.make_async_copy(ref.at[source], target, sems.at[index * pieces + at])
                )
        for copy in copies:
            copy.start()
        for copy in copies:
            copy.wait()

    return line.call(
        "ordered_rows",
        kernel,
        [flip, tokens, out_grad],
        [SCALAR, ANY, ANY],
        LOCAL,
        shaped(2, rows, width),
        limit=52,
        scratch_shapes=[pltpu.SemaphoreType.DMA((2 * pieces,))],
    )


def parted(line, value):
    _, rows, width = value.shape
    half = rows // 2

    def kernel(a_ref, *outs):
        for index, out in enumerate(outs):
            out[...] = a_ref[index // 2, index % 2 * half : (index % 2 + 1) * half]

    return line.call(
        "parted", kernel, [value], [LOCAL], [LOCAL] * 4, [shaped(half, width)] * 4, limit=4
    )


def pass_on(line, value):
    def kernel(a_ref, o_ref):
        pass

    return line.call(
        "pass_on",
        kernel,
        [value],
        [ANY],
        ANY,
        shaped(*value.shape),
        limit=1,
        input_output_aliases={0: 0},
    )


def forward_products(line, core, own, other, low, rows, piece, weights):
    width = own.shape[2]
    units = weights[0].shape[1]
    tile = min(256, units)

    def kernel(core_ref, own_ref, *refs):
        other_refs, (gate_ref, up_ref, down_ref, last_ref, first_ref) = refs[:4], refs[4:]
        here = pl.ds(pl.multiple_of(core_ref[0] * width, width), width)
        there = pl.ds(pl.multiple_of((1 - core_ref[0]) * width, width), width)

        @pl.loop(0, units // tile)
        def _(step):
            columns = pl.ds(pl.multiple_of(step * tile, tile), tile)
            for index, (which, weight) in enumerate(((0, gate_ref), (0, up_ref), (1, down_ref))):
                left = own_ref[which, low : low + rows]
                part = jnp.dot(left, weight[here, columns], preferred_element_type=F32)
                left = jnp.concatenate([ref[...] for ref in other_refs[2 * which : 2 * which + 2]])
                left = left[low : low + rows]
                part += jnp.dot(left, weight[there, columns], preferred_element_type=F32)
                part = part.astype(BF16)
                for at in range(0, rows // piece, 2):
                    to = slice(at // 2 * piece, (at // 2 + 1) * piece)
                    last_ref[index, to, columns] = part[at * piece : (at + 1) * piece]
                    first_ref[index, to, columns] = part[(at + 1) * piece : (at + 2) * piece]

    return line.call(
        "forward_products",
        kernel,
        [core, own, *other, *weights],
        [SCALAR] + [LOCAL] * 8,
        [LOCAL] * 2,
        [shaped(3, rows // 2, units)] * 2,
    )


def add_on(line, held, received):
    def kernel(a_ref, b_ref, o_ref):
        o_ref[...] = (a_ref[...].astype(F32) + b_ref[...].astype(F32)).astype(BF16)

    return line.call(
        "add_on", kernel, [held, received], [LOCAL] * 2, LOCAL, shaped(*held.shape), limit=4
    )


def add_quarters(line, held, quarters, apart):
    _, rows, width = held.shape
    half = rows // 2

    def kernel(a_ref, *refs):
        for index, ref in enumerate(refs[:4]):
            to = slice(index % 2 * half, (index % 2 + 1) * half)
            total = a_ref[index // 2, to].astype(F32) + ref[...].astype(F32)
            if apart:
                refs[4 + index // 2][0, to] = total.astype(BF16)
            else:
                refs[4][index // 2, to] = total.astype(BF16)

    return line.call(
        "add_quarters",
        kernel,
        [held, *quarters],
        [LOCAL] * 5,
        [LOCAL] * (1 + apart),
        [shaped(1, rows, width)] * 2 if apart else [shaped(*held.shape)],
        limit=4,
    )


def activations(line, held, received):
    def kernel(a_ref, b_ref, o_ref):
        gate, up, grad = [a_ref[i].astype(F32) + b_ref[i].astype(F32) for i in range(3)]
        sigmoid = jax.nn.sigmoid(gate)
        active = gate * sigmoid
        o_ref[0] = (active * up).astype(BF16)
        o_ref[1] = (grad * up * sigmoid * (1.0 + gate * (1.0 - sigmoid))).astype(BF16)
        o_ref[2] = (grad * active).astype(BF16)

    return line.call(
        "activations", kernel, [held, received], [LOCAL] * 2, LOCAL, shaped(*held.shape), limit=4
    )


def backward_products(line, core, place, passed, piece, weights):
    count = len(passed)
    _, half, units = passed[0].shape
    rows = 2 * half
    width = weights[0].shape[0] // 2

    def kernel(core_ref, place_ref, *refs):
        passed_refs = refs[:count]
        gate_ref, up_ref, down_ref, keep_ref, acts_ref = refs[count : count + 5]
        send_refs = refs[count + 5 :]
        near = jnp.minimum(place_ref[0], count - 1 - place_ref[0])
        for index, ref in enumerate(passed_refs):
            far = index >= count // 2

            @pl.when(near == (count - 1 - index if far else index))
            def _(ref=ref, far=far):
                for at in range(half // piece):
                    to = (2 * at + far) * piece
                    acts_ref[:, to : to + piece] = ref[:, at * piece : (at + 1) * piece]

        def fill(targets, side):
            lines = pl.ds(pl.multiple_of(side * width, width), width)
            out = lax.dot_general(down_ref[lines], acts_ref[0], NT, preferred_element_type=F32)
            grad = lax.dot_general(gate_ref[lines], acts_ref[1], NT, preferred_element_type=F32)
            grad += lax.dot_general(up_ref[lines], acts_ref[2], NT, preferred_element_type=F32)
            out, grad = out.astype(BF16).T, grad.astype(BF16).T
            if len(targets) == 1:
                targets[0][0], targets[0][1] = out, grad
            else:
                targets[0][...], targets[1][...] = out[:half], out[half:]
                targets[2][...], targets[3][...] = grad[:half], grad[half:]

        fill(send_refs, 1 - core_ref[0])
        fill([keep_ref], core_ref[0])

    return line.call(
        "backward_products",
        kernel,
        [core, place, *passed, *weights],
        [SCALAR] * 2 + [LOCAL] * (count + 3),
        [LOCAL] * 6,
        [shaped(2, rows, width), shaped(3, rows, units)] + [shaped(half, width)] * 4,
    )


def weight_grads(line, core, owns, others, acts, spans):
    count, chunks = len(owns), len(acts)
    _, rows, width = owns[0].shape
    units = acts[0].shape[2]
    tile = min(256, width)
    steps = width // tile
    total = rows * count
    slots = 3

    def kernel(core_ref, *refs):
        own_refs, other_refs = refs[:count], refs[count : 5 * count]
        act_refs = refs[5 * count : 5 * count + chunks]
        _, gate_out, up_out, down_out, all_acts, left, held, sems = refs[5 * count + chunks :]
        for ref, (low, high) in zip(act_refs, spans):
            all_acts[:, low:high] = ref[...]

        def copies(step, slot):
            side = jnp.where(step < steps, core_ref[0], 1 - core_ref[0])
            line_at = pl.multiple_of((side * steps + lax.rem(step, steps)) * tile, tile)
            return [
                pltpu.make_async_copy(
                    held.at[slot, index], out.at[pl.ds(line_at, tile)], sems.at[slot, index]
                )
                for index, out in enumerate((gate_out, up_out, down_out))
            ]

        @pl.loop(0, 2 * steps)
        def _(step):
            slot = lax.rem(step, slots)
            columns = pl.ds(pl.multiple_of(lax.rem(step, steps) * tile, tile), tile)

            @pl.when(step < steps)
            def _():
                for index, ref in enumerate(own_refs):
                    left[:, index * rows : (index + 1) * rows] = ref[:, :, columns]

            @pl.when(step >= steps)
            def _():
                for index, ref in enumerate(other_refs):
                    to = index // 4 * rows + index % 2 * (rows // 2)
                    left[index // 2 % 2, to : to + rows // 2] = ref[:, columns]

            @pl.when(step >= slots)
            def _():
                for copy in copies(step - slots, slot):
                    copy.wait()

            out_copies = copies(step, slot)
            for index, (which, act) in enumerate(((0, 1), (0, 2), (1, 0))):
                held[slot, index] = lax.dot_general(
                    left[which], all_acts[act], TN, preferred_element_type=F32
                )
                out_copies[index].start()

        for step in range(max(0, 2 * steps - slots), 2 * steps):
            for copy in copies(step, step % slots):
                copy.wait()

    return line.call(
        "weight_grads",
        kernel,
        [core, *owns, *[ref for quarters in others for ref in quarters], *acts],
        [SCALAR] + [LOCAL] * (5 * count + chunks),
        [ANY] * 4,
        [shaped(16, 128)] + [shaped(2 * width, units, dtype=F32)] * 3,
        limit=32,
        scratch_shapes=[
            pltpu.VMEM((3, total, units), BF16),
            pltpu.VMEM((2, total, tile), BF16),
            pltpu.VMEM((slots, 3, tile, units), F32),
            pltpu.SemaphoreType.DMA((slots, 3)),
        ],
    )


def final_sum(line, parts, flip, piece):
    rows = sum(part[0].shape[1] for part in parts[0])
    width = parts[0][0][0].shape[2]
    flat = [half for block in parts for part in block for half in part]

    def kernel(flip_ref, *refs):
        outs = refs[len(flat) :]
        at = 0
        sources = []
        for block in parts:
            spans = []
            for part in block:
                ends = [(refs[at + i * (len(part) - 1)], i * (2 - len(part))) for i in range(2)]
                at += len(part)
                spans += [(ends, low) for low in range(0, part[0].shape[1], piece)]
            sources.append(spans)
        for place in range(rows // piece):
            to = pl.ds(pl.multiple_of((place ^ flip_ref[0]) * piece, piece), piece)
            for index, out_ref in enumerate(outs):
                total = 0.0
                for spans in sources:
                    ends, low = spans[place]
                    ref, which = ends[index]
                    total += ref[which, low : low + piece].astype(F32)
                out_ref[to] = total.astype(BF16)

    return line.call(
        "final_sum",
        kernel,
        [flip, *flat],
        [SCALAR] + [LOCAL] * len(flat),
        [LOCAL] * 2,
        [shaped(rows, width)] * 2,
    )


WEIGHTS = -1
FOUR = (
    0, 1, 2, 1, 2, 0, 3, 1, 0, 3, 2, 1, 0, 3, 2, 1, 0, 3, 2, 1,
    0, 3, 2, 1, 0, 3, 2, 0, 1, 1, 3, 2, 1, 2, 2, 3, 3, 3, WEIGHTS, 0,
    1, 2, 3,
)


def plan_of(n_gy, n_gz, pieces):
    if (n_gy, n_gz) == (4, 4):
        return [(d, 0, pieces) for d in (0, 1, 2, 3)], FOUR
    chunks = [(d, 0, pieces) for d in range(n_gy)]
    events = []
    for at, (d, _, _) in enumerate(chunks):
        for k in range(-1 if d else 0, 2 * n_gz + (2 if d else 1)):
            events.append((at + 2 * k, at))
    return chunks, [at for _, at in sorted(events)] + [WEIGHTS]


def per_device(sizes, tokens, gate_weight, up_weight, down_weight, out_grad):
    n_gy, n_gz = sizes["gy"], sizes["gz"]
    pieces = 4
    piece = tokens.shape[0] // pieces
    core = lax.axis_index("gx").astype(jnp.int32).reshape(1)
    level = lax.axis_index("gz").astype(jnp.int32)
    place = level.reshape(1)
    flip = (level >= n_gz // 2).astype(jnp.int32).reshape(1)

    def swap_core(quarters):
        return [swap(quarter, "gx", 2, 1) for quarter in quarters]
    line = Line()

    def hop(value, step):
        pairs = [(step, step + 1), (n_gz - 1 - step, n_gz - 2 - step)]
        return lax.ppermute(value, "gz", pairs)

    mine = ordered_rows(line, tokens, out_grad, flip, pieces)
    others = [swap_core(parted(line, mine))] + [None] * (n_gy - 1)
    owns = {0: mine}

    def send_blocks(d):
        step = 1 << d.bit_length()
        while step < n_gy:
            owns[d | step] = swap(owns[d], "gy", n_gy, step)
            step <<= 1

    send_blocks(0)
    weights = (gate_weight, up_weight, down_weight)
    acts = {}

    def chunk(at, d, first_piece, count):
        if others[d] is None:
            yield
            owns[d] = pass_on(line, owns[d])
            others[d] = swap_core(parted(line, owns[d]))
            send_blocks(d)
        yield
        last, first = forward_products(
            line, core, owns[d], others[d], first_piece * piece, count * piece, piece, weights
        )
        value = first
        for step in range(n_gz - 1):
            got = hop(value, step)
            yield
            if step < n_gz - 2:
                value = add_on(line, first if step + 1 < n_gz // 2 else last, got)
        value = activations(line, last, got)
        passed = [value]
        for step in range(n_gz - 1):
            value = hop(value, step)
            yield
            value = pass_on(line, value)
            passed.append(value)
        yield
        keep, acts[at], *send = backward_products(line, core, place, passed, piece, weights)
        got = swap_core(send)
        yield
        part = add_quarters(line, keep, got, at == len(plan) - 1)
        if d:
            part = [swap(half, "gy", n_gy, d) for half in part]
            yield
            part = [pass_on(line, half) for half in part]
        parts[d].append(part)
        yield

    plan, order = plan_of(n_gy, n_gz, pieces)
    spans = []
    for d, first_piece, count in plan:
        low = (d * pieces + first_piece) * piece
        spans.append((low, low + count * piece))
    parts = [[] for _ in range(n_gy)]
    runs = [chunk(at, *entry) for at, entry in enumerate(plan)]
    for run in runs:
        next(run)
    for at in order:
        if at == WEIGHTS:
            every = [acts[i] for i in range(len(plan))]
            grads = weight_grads(
                line, core, [owns[d] for d in range(n_gy)], others, every, spans
            )
        else:
            next(runs[at])
    output, tokens_grad = final_sum(line, parts, flip, piece)
    _, gate_grad_w, up_grad_w, down_grad_w = grads
    return (output, tokens_grad, gate_grad_w, up_grad_w, down_grad_w)


def solution(mesh):
    return jax.shard_map(
        functools.partial(per_device, dict(mesh.shape)),
        mesh=mesh,
        in_specs=(
            P("gy", ("gz", "gx")),
            P("gz", ("gx", "gy")),
            P("gz", ("gx", "gy")),
            P("gz", ("gx", "gy")),
            P("gy", ("gz", "gx")),
        ),
        out_specs=(
            P("gy", ("gz", "gx")),
            P("gy", ("gz", "gx")),
            P("gz", ("gx", "gy")),
            P("gz", ("gx", "gy")),
            P("gz", ("gx", "gy")),
        ),
        check_vma=False,
    )
```

```python
import functools

import jax
import jax.numpy as jnp
from jax import lax
from jax.experimental import pallas as pl
from jax.experimental.pallas import tpu as pltpu
from jax.sharding import PartitionSpec as P

BF16 = jnp.bfloat16
F32 = jnp.float32
MIB = 1 << 20
NT = (((1,), (1,)), ((), ()))
TN = (((0,), (0,)), ((), ()))
LOCAL = pl.BlockSpec(memory_space=pltpu.VMEM)
SCALAR = pl.BlockSpec(memory_space=pltpu.SMEM)
ANY = pl.BlockSpec(memory_space=pl.ANY)


def shaped(*dims, dtype=BF16):
    return jax.ShapeDtypeStruct(dims, dtype)


class Line:
    def __init__(self):
        self.last = None

    def call(self, name, kernel, operands, in_specs, out_specs, out_shape, limit=16, cost=1000, **rest):
        if self.last is not None:
            count, inner = len(operands), kernel
            operands, in_specs = [*operands, self.last], [*in_specs, ANY]

            def kernel(*refs):
                inner(*refs[:count], *refs[count + 1 :])

        result = pl.pallas_call(
            kernel,
            in_specs=in_specs,
            out_specs=out_specs,
            out_shape=out_shape,
            compiler_params=pltpu.CompilerParams(vmem_limit_bytes=limit * MIB),
            cost_estimate=pl.CostEstimate(flops=1000, bytes_accessed=cost, transcendentals=0),
            name=name,
            **rest,
        )(*operands)
        self.last = result[0] if isinstance(result, (list, tuple)) else result
        return result


def swap(value, axis, size, mask):
    return lax.ppermute(value, axis, [(i, i ^ mask) for i in range(size)])


def ordered_rows(line, tokens, out_grad, flip, pieces):
    rows, width = tokens.shape
    piece = rows // pieces

    def kernel(flip_ref, a_ref, b_ref, o_ref, sems):
        copies = []
        for index, ref in enumerate((a_ref, b_ref)):
            for at in range(pieces):
                source = pl.ds(pl.multiple_of((at ^ flip_ref[0]) * piece, piece), piece)
                target = o_ref.at[index, at * piece : (at + 1) * piece]
                copies.append(
                    pltpu.make_async_copy(ref.at[source], target, sems.at[index * pieces + at])
                )
        for copy in copies:
            copy.start()
        for copy in copies:
            copy.wait()

    return line.call(
        "ordered_rows",
        kernel,
        [flip, tokens, out_grad],
        [SCALAR, ANY, ANY],
        LOCAL,
        shaped(2, rows, width),
        limit=52,
        scratch_shapes=[pltpu.SemaphoreType.DMA((2 * pieces,))],
    )


def parted(line, value):
    _, rows, width = value.shape
    half = rows // 2

    def kernel(a_ref, *outs):
        for index, out in enumerate(outs):
            out[...] = a_ref[index // 2, index % 2 * half : (index % 2 + 1) * half]

    return line.call(
        "parted", kernel, [value], [LOCAL], [LOCAL] * 4, [shaped(half, width)] * 4, limit=4
    )


def pass_on(line, value):
    def kernel(a_ref, o_ref):
        pass

    return line.call(
        "pass_on",
        kernel,
        [value],
        [ANY],
        ANY,
        shaped(*value.shape),
        limit=1,
        input_output_aliases={0: 0},
    )


def forward_products(line, core, own, other, low, rows, piece, weights):
    width = own.shape[2]
    units = weights[0].shape[1]
    tile = min(256, units)

    def kernel(core_ref, own_ref, *refs):
        other_refs, (gate_ref, up_ref, down_ref, last_ref, first_ref) = refs[:4], refs[4:]
        here = pl.ds(pl.multiple_of(core_ref[0] * width, width), width)
        there = pl.ds(pl.multiple_of((1 - core_ref[0]) * width, width), width)

        @pl.loop(0, units // tile)
        def _(step):
            columns = pl.ds(pl.multiple_of(step * tile, tile), tile)
            for index, (which, weight) in enumerate(((0, gate_ref), (0, up_ref), (1, down_ref))):
                left = own_ref[which, low : low + rows]
                part = jnp.dot(left, weight[here, columns], preferred_element_type=F32)
                left = jnp.concatenate([ref[...] for ref in other_refs[2 * which : 2 * which + 2]])
                left = left[low : low + rows]
                part += jnp.dot(left, weight[there, columns], preferred_element_type=F32)
                part = part.astype(BF16)
                for at in range(0, rows // piece, 2):
                    to = slice(at // 2 * piece, (at // 2 + 1) * piece)
                    last_ref[index, to, columns] = part[at * piece : (at + 1) * piece]
                    first_ref[index, to, columns] = part[(at + 1) * piece : (at + 2) * piece]

    return line.call(
        "forward_products",
        kernel,
        [core, own, *other, *weights],
        [SCALAR] + [LOCAL] * 8,
        [LOCAL] * 2,
        [shaped(3, rows // 2, units)] * 2,
    )


def add_on(line, held, received):
    def kernel(a_ref, b_ref, o_ref):
        o_ref[...] = (a_ref[...].astype(F32) + b_ref[...].astype(F32)).astype(BF16)

    return line.call(
        "add_on", kernel, [held, received], [LOCAL] * 2, LOCAL, shaped(*held.shape), limit=4
    )


def add_quarters(line, held, quarters, apart):
    _, rows, width = held.shape
    half = rows // 2

    def kernel(a_ref, *refs):
        for index, ref in enumerate(refs[:4]):
            to = slice(index % 2 * half, (index % 2 + 1) * half)
            total = a_ref[index // 2, to].astype(F32) + ref[...].astype(F32)
            if apart:
                refs[4 + index // 2][0, to] = total.astype(BF16)
            else:
                refs[4][index // 2, to] = total.astype(BF16)

    return line.call(
        "add_quarters",
        kernel,
        [held, *quarters],
        [LOCAL] * 5,
        [LOCAL] * (1 + apart),
        [shaped(1, rows, width)] * 2 if apart else [shaped(*held.shape)],
        limit=4,
    )


def activations(line, held, received):
    def kernel(a_ref, b_ref, o_ref):
        gate, up, grad = [a_ref[i].astype(F32) + b_ref[i].astype(F32) for i in range(3)]
        sigmoid = jax.nn.sigmoid(gate)
        active = gate * sigmoid
        o_ref[0] = (active * up).astype(BF16)
        o_ref[1] = (grad * up * sigmoid * (1.0 + gate * (1.0 - sigmoid))).astype(BF16)
        o_ref[2] = (grad * active).astype(BF16)

    return line.call(
        "activations", kernel, [held, received], [LOCAL] * 2, LOCAL, shaped(*held.shape), limit=4
    )


def backward_products(line, core, place, passed, piece, weights):
    count = len(passed)
    _, half, units = passed[0].shape
    rows = 2 * half
    width = weights[0].shape[0] // 2

    def kernel(core_ref, place_ref, *refs):
        passed_refs = refs[:count]
        gate_ref, up_ref, down_ref, keep_ref, acts_ref = refs[count : count + 5]
        send_refs = refs[count + 5 :]
        near = jnp.minimum(place_ref[0], count - 1 - place_ref[0])
        for index, ref in enumerate(passed_refs):
            far = index >= count // 2

            @pl.when(near == (count - 1 - index if far else index))
            def _(ref=ref, far=far):
                for at in range(half // piece):
                    to = (2 * at + far) * piece
                    acts_ref[:, to : to + piece] = ref[:, at * piece : (at + 1) * piece]

        def fill(targets, side):
            lines = pl.ds(pl.multiple_of(side * width, width), width)
            out = lax.dot_general(down_ref[lines], acts_ref[0], NT, preferred_element_type=F32)
            grad = lax.dot_general(gate_ref[lines], acts_ref[1], NT, preferred_element_type=F32)
            grad += lax.dot_general(up_ref[lines], acts_ref[2], NT, preferred_element_type=F32)
            out, grad = out.astype(BF16).T, grad.astype(BF16).T
            if len(targets) == 1:
                targets[0][0], targets[0][1] = out, grad
            else:
                targets[0][...], targets[1][...] = out[:half], out[half:]
                targets[2][...], targets[3][...] = grad[:half], grad[half:]

        fill(send_refs, 1 - core_ref[0])
        fill([keep_ref], core_ref[0])

    return line.call(
        "backward_products",
        kernel,
        [core, place, *passed, *weights],
        [SCALAR] * 2 + [LOCAL] * (count + 3),
        [LOCAL] * 6,
        [shaped(2, rows, width), shaped(3, rows, units)] + [shaped(half, width)] * 4,
    )


def weight_grads(line, core, owns, others, acts, spans):
    count, chunks = len(owns), len(acts)
    _, rows, width = owns[0].shape
    units = acts[0].shape[2]
    tile = min(256, width)
    steps = width // tile
    total = rows * count
    slots = 3

    def kernel(core_ref, *refs):
        own_refs, other_refs = refs[:count], refs[count : 5 * count]
        act_refs = refs[5 * count : 5 * count + chunks]
        _, gate_out, up_out, down_out, all_acts, left, held, sems = refs[5 * count + chunks :]
        for ref, (low, high) in zip(act_refs, spans):
            all_acts[:, low:high] = ref[...]

        def copies(step, slot):
            side = jnp.where(step < steps, core_ref[0], 1 - core_ref[0])
            line_at = pl.multiple_of((side * steps + lax.rem(step, steps)) * tile, tile)
            return [
                pltpu.make_async_copy(
                    held.at[slot, index], out.at[pl.ds(line_at, tile)], sems.at[slot, index]
                )
                for index, out in enumerate((gate_out, up_out, down_out))
            ]

        @pl.loop(0, 2 * steps)
        def _(step):
            slot = lax.rem(step, slots)
            columns = pl.ds(pl.multiple_of(lax.rem(step, steps) * tile, tile), tile)

            @pl.when(step < steps)
            def _():
                for index, ref in enumerate(own_refs):
                    left[:, index * rows : (index + 1) * rows] = ref[:, :, columns]

            @pl.when(step >= steps)
            def _():
                for index, ref in enumerate(other_refs):
                    to = index // 4 * rows + index % 2 * (rows // 2)
                    left[index // 2 % 2, to : to + rows // 2] = ref[:, columns]

            @pl.when(step >= slots)
            def _():
                for copy in copies(step - slots, slot):
                    copy.wait()

            out_copies = copies(step, slot)
            for index, (which, act) in enumerate(((0, 1), (0, 2), (1, 0))):
                held[slot, index] = lax.dot_general(
                    left[which], all_acts[act], TN, preferred_element_type=F32
                )
                out_copies[index].start()

        for step in range(max(0, 2 * steps - slots), 2 * steps):
            for copy in copies(step, step % slots):
                copy.wait()

    return line.call(
        "weight_grads",
        kernel,
        [core, *owns, *[ref for quarters in others for ref in quarters], *acts],
        [SCALAR] + [LOCAL] * (5 * count + chunks),
        [ANY] * 4,
        [shaped(16, 128)] + [shaped(2 * width, units, dtype=F32)] * 3,
        limit=32,
        scratch_shapes=[
            pltpu.VMEM((3, total, units), BF16),
            pltpu.VMEM((2, total, tile), BF16),
            pltpu.VMEM((slots, 3, tile, units), F32),
            pltpu.SemaphoreType.DMA((slots, 3)),
        ],
    )


def final_sum(line, parts, flip, piece):
    rows = sum(part[0].shape[1] for part in parts[0])
    width = parts[0][0][0].shape[2]
    flat = [half for block in parts for part in block for half in part]

    def kernel(flip_ref, *refs):
        outs = refs[len(flat) :]
        at = 0
        sources = []
        for block in parts:
            spans = []
            for part in block:
                ends = [(refs[at + i * (len(part) - 1)], i * (2 - len(part))) for i in range(2)]
                at += len(part)
                spans += [(ends, low) for low in range(0, part[0].shape[1], piece)]
            sources.append(spans)
        for place in range(rows // piece):
            to = pl.ds(pl.multiple_of((place ^ flip_ref[0]) * piece, piece), piece)
            for index, out_ref in enumerate(outs):
                total = 0.0
                for spans in sources:
                    ends, low = spans[place]
                    ref, which = ends[index]
                    total += ref[which, low : low + piece].astype(F32)
                out_ref[to] = total.astype(BF16)

    return line.call(
        "final_sum",
        kernel,
        [flip, *flat],
        [SCALAR] + [LOCAL] * len(flat),
        [LOCAL] * 2,
        [shaped(rows, width)] * 2,
    )


WEIGHTS = -1
FOUR = (
    0, 1, 2, 1, 2, 0, 3, 1, 0, 3, 2, 1, 0, 3, 2, 1, 0, 3, 2, 1,
    0, 3, 2, 1, 0, 3, 2, 0, 1, 3, 1, 1, 2, 2, 3, 2, 3, 1, 3, 0,
    WEIGHTS, 2, 3,
)


def plan_of(n_gy, n_gz, pieces):
    if (n_gy, n_gz) == (4, 4):
        return [(d, 0, pieces) for d in (0, 1, 2, 3)], FOUR
    chunks = [(d, 0, pieces) for d in range(n_gy)]
    events = []
    for at, (d, _, _) in enumerate(chunks):
        for k in range(-1 if d else 0, 2 * n_gz + (2 if d else 1)):
            events.append((at + 2 * k, at))
    return chunks, [at for _, at in sorted(events)] + [WEIGHTS]


def per_device(sizes, tokens, gate_weight, up_weight, down_weight, out_grad):
    n_gy, n_gz = sizes["gy"], sizes["gz"]
    pieces = 4
    piece = tokens.shape[0] // pieces
    core = lax.axis_index("gx").astype(jnp.int32).reshape(1)
    level = lax.axis_index("gz").astype(jnp.int32)
    place = level.reshape(1)
    flip = (level >= n_gz // 2).astype(jnp.int32).reshape(1)

    def swap_core(quarters):
        return [swap(quarter, "gx", 2, 1) for quarter in quarters]
    line = Line()

    def hop(value, step):
        pairs = [(step, step + 1), (n_gz - 1 - step, n_gz - 2 - step)]
        return lax.ppermute(value, "gz", pairs)

    mine = ordered_rows(line, tokens, out_grad, flip, pieces)
    others = [swap_core(parted(line, mine))] + [None] * (n_gy - 1)
    owns = {0: mine}

    def send_blocks(d):
        step = 1 << d.bit_length()
        while step < n_gy:
            owns[d | step] = swap(owns[d], "gy", n_gy, step)
            step <<= 1

    send_blocks(0)
    weights = (gate_weight, up_weight, down_weight)
    acts = {}

    def chunk(at, d, first_piece, count):
        if others[d] is None:
            yield
            owns[d] = pass_on(line, owns[d])
            others[d] = swap_core(parted(line, owns[d]))
            send_blocks(d)
        yield
        last, first = forward_products(
            line, core, owns[d], others[d], first_piece * piece, count * piece, piece, weights
        )
        value = first
        for step in range(n_gz - 1):
            got = hop(value, step)
            yield
            if step < n_gz - 2:
                value = add_on(line, first if step + 1 < n_gz // 2 else last, got)
        value = activations(line, last, got)
        passed = [value]
        for step in range(n_gz - 1):
            value = hop(value, step)
            yield
            value = pass_on(line, value)
            passed.append(value)
        yield
        keep, acts[at], *send = backward_products(line, core, place, passed, piece, weights)
        got = swap_core(send)
        yield
        part = add_quarters(line, keep, got, at == len(plan) - 1)
        if d:
            part = [swap(half, "gy", n_gy, d) for half in part]
            yield
            part = [pass_on(line, half) for half in part]
        parts[d].append(part)
        yield

    plan, order = plan_of(n_gy, n_gz, pieces)
    spans = []
    for d, first_piece, count in plan:
        low = (d * pieces + first_piece) * piece
        spans.append((low, low + count * piece))
    parts = [[] for _ in range(n_gy)]
    runs = [chunk(at, *entry) for at, entry in enumerate(plan)]
    for run in runs:
        next(run)
    for at in order:
        if at == WEIGHTS:
            every = [acts[i] for i in range(len(plan))]
            grads = weight_grads(
                line, core, [owns[d] for d in range(n_gy)], others, every, spans
            )
        else:
            next(runs[at])
    output, tokens_grad = final_sum(line, parts, flip, piece)
    _, gate_grad_w, up_grad_w, down_grad_w = grads
    return (output, tokens_grad, gate_grad_w, up_grad_w, down_grad_w)


def solution(mesh):
    return jax.shard_map(
        functools.partial(per_device, dict(mesh.shape)),
        mesh=mesh,
        in_specs=(
            P("gy", ("gz", "gx")),
            P("gz", ("gx", "gy")),
            P("gz", ("gx", "gy")),
            P("gz", ("gx", "gy")),
            P("gy", ("gz", "gx")),
        ),
        out_specs=(
            P("gy", ("gz", "gx")),
            P("gy", ("gz", "gx")),
            P("gz", ("gx", "gy")),
            P("gz", ("gx", "gy")),
            P("gz", ("gx", "gy")),
        ),
        check_vma=False,
    )
```

```python
import functools

import jax
import jax.numpy as jnp
from jax import lax
from jax.experimental import pallas as pl
from jax.experimental.pallas import tpu as pltpu
from jax.sharding import PartitionSpec as P

BF16 = jnp.bfloat16
F32 = jnp.float32
MIB = 1 << 20
NT = (((1,), (1,)), ((), ()))
TN = (((0,), (0,)), ((), ()))
LOCAL = pl.BlockSpec(memory_space=pltpu.VMEM)
SCALAR = pl.BlockSpec(memory_space=pltpu.SMEM)
ANY = pl.BlockSpec(memory_space=pl.ANY)


def shaped(*dims, dtype=BF16):
    return jax.ShapeDtypeStruct(dims, dtype)


class Line:
    def __init__(self):
        self.last = None

    def call(self, name, kernel, operands, in_specs, out_specs, out_shape, limit=16, cost=1000, **rest):
        if self.last is not None:
            count, inner = len(operands), kernel
            operands, in_specs = [*operands, self.last], [*in_specs, ANY]

            def kernel(*refs):
                inner(*refs[:count], *refs[count + 1 :])

        result = pl.pallas_call(
            kernel,
            in_specs=in_specs,
            out_specs=out_specs,
            out_shape=out_shape,
            compiler_params=pltpu.CompilerParams(vmem_limit_bytes=limit * MIB),
            cost_estimate=pl.CostEstimate(flops=1000, bytes_accessed=cost, transcendentals=0),
            name=name,
            **rest,
        )(*operands)
        self.last = result[0] if isinstance(result, (list, tuple)) else result
        return result


def swap(value, axis, size, mask):
    return lax.ppermute(value, axis, [(i, i ^ mask) for i in range(size)])


def ordered_rows(line, tokens, out_grad, flip, pieces):
    rows, width = tokens.shape
    piece = rows // pieces

    def kernel(flip_ref, a_ref, b_ref, o_ref, sems):
        copies = []
        for index, ref in enumerate((a_ref, b_ref)):
            for at in range(pieces):
                source = pl.ds(pl.multiple_of((at ^ flip_ref[0]) * piece, piece), piece)
                target = o_ref.at[index, at * piece : (at + 1) * piece]
                copies.append(
                    pltpu.make_async_copy(ref.at[source], target, sems.at[index * pieces + at])
                )
        for copy in copies:
            copy.start()
        for copy in copies:
            copy.wait()

    return line.call(
        "ordered_rows",
        kernel,
        [flip, tokens, out_grad],
        [SCALAR, ANY, ANY],
        LOCAL,
        shaped(2, rows, width),
        limit=52,
        scratch_shapes=[pltpu.SemaphoreType.DMA((2 * pieces,))],
    )


def parted(line, value):
    _, rows, width = value.shape
    half = rows // 2

    def kernel(a_ref, *outs):
        for index, out in enumerate(outs):
            out[...] = a_ref[index // 2, index % 2 * half : (index % 2 + 1) * half]

    return line.call(
        "parted", kernel, [value], [LOCAL], [LOCAL] * 4, [shaped(half, width)] * 4, limit=4
    )


def pass_on(line, value):
    def kernel(a_ref, o_ref):
        pass

    return line.call(
        "pass_on",
        kernel,
        [value],
        [ANY],
        ANY,
        shaped(*value.shape),
        limit=1,
        input_output_aliases={0: 0},
    )


def forward_products(line, core, own, other, low, rows, piece, weights):
    width = own.shape[2]
    units = weights[0].shape[1]
    tile = min(256, units)

    def kernel(core_ref, own_ref, *refs):
        other_refs, (gate_ref, up_ref, down_ref, last_ref, first_ref) = refs[:4], refs[4:]
        here = pl.ds(pl.multiple_of(core_ref[0] * width, width), width)
        there = pl.ds(pl.multiple_of((1 - core_ref[0]) * width, width), width)

        @pl.loop(0, units // tile)
        def _(step):
            columns = pl.ds(pl.multiple_of(step * tile, tile), tile)
            for index, (which, weight) in enumerate(((0, gate_ref), (0, up_ref), (1, down_ref))):
                left = own_ref[which, low : low + rows]
                part = jnp.dot(left, weight[here, columns], preferred_element_type=F32)
                left = jnp.concatenate([ref[...] for ref in other_refs[2 * which : 2 * which + 2]])
                left = left[low : low + rows]
                part += jnp.dot(left, weight[there, columns], preferred_element_type=F32)
                part = part.astype(BF16)
                for at in range(0, rows // piece, 2):
                    to = slice(at // 2 * piece, (at // 2 + 1) * piece)
                    last_ref[index, to, columns] = part[at * piece : (at + 1) * piece]
                    first_ref[index, to, columns] = part[(at + 1) * piece : (at + 2) * piece]

    return line.call(
        "forward_products",
        kernel,
        [core, own, *other, *weights],
        [SCALAR] + [LOCAL] * 8,
        [LOCAL] * 2,
        [shaped(3, rows // 2, units)] * 2,
    )


def add_on(line, held, received):
    def kernel(a_ref, b_ref, o_ref):
        o_ref[...] = (a_ref[...].astype(F32) + b_ref[...].astype(F32)).astype(BF16)

    return line.call(
        "add_on", kernel, [held, received], [LOCAL] * 2, LOCAL, shaped(*held.shape), limit=4
    )


def add_quarters(line, held, quarters, apart):
    _, rows, width = held.shape
    half = rows // 2

    def kernel(a_ref, *refs):
        for index, ref in enumerate(refs[:4]):
            to = slice(index % 2 * half, (index % 2 + 1) * half)
            total = a_ref[index // 2, to].astype(F32) + ref[...].astype(F32)
            if apart:
                refs[4 + index // 2][0, to] = total.astype(BF16)
            else:
                refs[4][index // 2, to] = total.astype(BF16)

    return line.call(
        "add_quarters",
        kernel,
        [held, *quarters],
        [LOCAL] * 5,
        [LOCAL] * (1 + apart),
        [shaped(1, rows, width)] * 2 if apart else [shaped(*held.shape)],
        limit=4,
    )


def activations(line, held, received):
    def kernel(a_ref, b_ref, o_ref):
        gate, up, grad = [a_ref[i].astype(F32) + b_ref[i].astype(F32) for i in range(3)]
        sigmoid = jax.nn.sigmoid(gate)
        active = gate * sigmoid
        o_ref[0] = (active * up).astype(BF16)
        o_ref[1] = (grad * up * sigmoid * (1.0 + gate * (1.0 - sigmoid))).astype(BF16)
        o_ref[2] = (grad * active).astype(BF16)

    return line.call(
        "activations", kernel, [held, received], [LOCAL] * 2, LOCAL, shaped(*held.shape), limit=4
    )


def backward_products(line, core, place, passed, piece, weights):
    count = len(passed)
    _, half, units = passed[0].shape
    rows = 2 * half
    width = weights[0].shape[0] // 2

    def kernel(core_ref, place_ref, *refs):
        passed_refs = refs[:count]
        gate_ref, up_ref, down_ref, keep_ref, acts_ref = refs[count : count + 5]
        send_refs = refs[count + 5 :]
        near = jnp.minimum(place_ref[0], count - 1 - place_ref[0])
        for index, ref in enumerate(passed_refs):
            far = index >= count // 2

            @pl.when(near == (count - 1 - index if far else index))
            def _(ref=ref, far=far):
                for at in range(half // piece):
                    to = (2 * at + far) * piece
                    acts_ref[:, to : to + piece] = ref[:, at * piece : (at + 1) * piece]

        def fill(targets, side):
            lines = pl.ds(pl.multiple_of(side * width, width), width)
            out = lax.dot_general(down_ref[lines], acts_ref[0], NT, preferred_element_type=F32)
            grad = lax.dot_general(gate_ref[lines], acts_ref[1], NT, preferred_element_type=F32)
            grad += lax.dot_general(up_ref[lines], acts_ref[2], NT, preferred_element_type=F32)
            out, grad = out.astype(BF16).T, grad.astype(BF16).T
            if len(targets) == 1:
                targets[0][0], targets[0][1] = out, grad
            else:
                targets[0][...], targets[1][...] = out[:half], out[half:]
                targets[2][...], targets[3][...] = grad[:half], grad[half:]

        fill(send_refs, 1 - core_ref[0])
        fill([keep_ref], core_ref[0])

    return line.call(
        "backward_products",
        kernel,
        [core, place, *passed, *weights],
        [SCALAR] * 2 + [LOCAL] * (count + 3),
        [LOCAL] * 6,
        [shaped(2, rows, width), shaped(3, rows, units)] + [shaped(half, width)] * 4,
    )


def weight_grads(line, core, owns, others, acts, spans):
    count, chunks = len(owns), len(acts)
    _, rows, width = owns[0].shape
    units = acts[0].shape[2]
    tile = min(256, width)
    steps = width // tile
    total = rows * count
    slots = 3

    def kernel(core_ref, *refs):
        own_refs, other_refs = refs[:count], refs[count : 5 * count]
        act_refs = refs[5 * count : 5 * count + chunks]
        _, gate_out, up_out, down_out, all_acts, left, held, sems = refs[5 * count + chunks :]
        for ref, (low, high) in zip(act_refs, spans):
            all_acts[:, low:high] = ref[...]

        def copies(step, slot):
            side = jnp.where(step < steps, core_ref[0], 1 - core_ref[0])
            line_at = pl.multiple_of((side * steps + lax.rem(step, steps)) * tile, tile)
            return [
                pltpu.make_async_copy(
                    held.at[slot, index], out.at[pl.ds(line_at, tile)], sems.at[slot, index]
                )
                for index, out in enumerate((gate_out, up_out, down_out))
            ]

        @pl.loop(0, 2 * steps)
        def _(step):
            slot = lax.rem(step, slots)
            columns = pl.ds(pl.multiple_of(lax.rem(step, steps) * tile, tile), tile)

            @pl.when(step < steps)
            def _():
                for index, ref in enumerate(own_refs):
                    left[:, index * rows : (index + 1) * rows] = ref[:, :, columns]

            @pl.when(step >= steps)
            def _():
                for index, ref in enumerate(other_refs):
                    to = index // 4 * rows + index % 2 * (rows // 2)
                    left[index // 2 % 2, to : to + rows // 2] = ref[:, columns]

            @pl.when(step >= slots)
            def _():
                for copy in copies(step - slots, slot):
                    copy.wait()

            out_copies = copies(step, slot)
            for index, (which, act) in enumerate(((0, 1), (0, 2), (1, 0))):
                held[slot, index] = lax.dot_general(
                    left[which], all_acts[act], TN, preferred_element_type=F32
                )
                out_copies[index].start()

        for step in range(max(0, 2 * steps - slots), 2 * steps):
            for copy in copies(step, step % slots):
                copy.wait()

    return line.call(
        "weight_grads",
        kernel,
        [core, *owns, *[ref for quarters in others for ref in quarters], *acts],
        [SCALAR] + [LOCAL] * (5 * count + chunks),
        [ANY] * 4,
        [shaped(16, 128)] + [shaped(2 * width, units, dtype=F32)] * 3,
        limit=32,
        scratch_shapes=[
            pltpu.VMEM((3, total, units), BF16),
            pltpu.VMEM((2, total, tile), BF16),
            pltpu.VMEM((slots, 3, tile, units), F32),
            pltpu.SemaphoreType.DMA((slots, 3)),
        ],
    )


def final_sum(line, parts, flip, piece):
    rows = sum(part[0].shape[1] for part in parts[0])
    width = parts[0][0][0].shape[2]
    flat = [half for block in parts for part in block for half in part]

    def kernel(flip_ref, *refs):
        outs = refs[len(flat) :]
        at = 0
        sources = []
        for block in parts:
            spans = []
            for part in block:
                ends = [(refs[at + i * (len(part) - 1)], i * (2 - len(part))) for i in range(2)]
                at += len(part)
                spans += [(ends, low) for low in range(0, part[0].shape[1], piece)]
            sources.append(spans)
        for place in range(rows // piece):
            to = pl.ds(pl.multiple_of((place ^ flip_ref[0]) * piece, piece), piece)
            for index, out_ref in enumerate(outs):
                total = 0.0
                for spans in sources:
                    ends, low = spans[place]
                    ref, which = ends[index]
                    total += ref[which, low : low + piece].astype(F32)
                out_ref[to] = total.astype(BF16)

    return line.call(
        "final_sum",
        kernel,
        [flip, *flat],
        [SCALAR] + [LOCAL] * len(flat),
        [LOCAL] * 2,
        [shaped(rows, width)] * 2,
    )


WEIGHTS = -1
FOUR = (
    0, 1, 2, 1, 2, 0, 3, 1, 0, 3, 2, 1, 0, 3, 2, 1, 0, 3, 2, 1,
    0, 3, 2, 1, 0, 3, 2, 0, 1, 1, 3, 2, 1, 2, 2, 3, 3, 1, 3, 2,
    WEIGHTS, 0, 3,
)


def plan_of(n_gy, n_gz, pieces):
    if (n_gy, n_gz) == (4, 4):
        return [(d, 0, pieces) for d in (0, 1, 2, 3)], FOUR
    chunks = [(d, 0, pieces) for d in range(n_gy)]
    events = []
    for at, (d, _, _) in enumerate(chunks):
        for k in range(-1 if d else 0, 2 * n_gz + (2 if d else 1)):
            events.append((at + 2 * k, at))
    return chunks, [at for _, at in sorted(events)] + [WEIGHTS]


def per_device(sizes, tokens, gate_weight, up_weight, down_weight, out_grad):
    n_gy, n_gz = sizes["gy"], sizes["gz"]
    pieces = 4
    piece = tokens.shape[0] // pieces
    core = lax.axis_index("gx").astype(jnp.int32).reshape(1)
    level = lax.axis_index("gz").astype(jnp.int32)
    place = level.reshape(1)
    flip = (level >= n_gz // 2).astype(jnp.int32).reshape(1)

    def swap_core(quarters):
        return [swap(quarter, "gx", 2, 1) for quarter in quarters]
    line = Line()

    def hop(value, step):
        pairs = [(step, step + 1), (n_gz - 1 - step, n_gz - 2 - step)]
        return lax.ppermute(value, "gz", pairs)

    mine = ordered_rows(line, tokens, out_grad, flip, pieces)
    others = [swap_core(parted(line, mine))] + [None] * (n_gy - 1)
    owns = {0: mine}

    def send_blocks(d):
        step = 1 << d.bit_length()
        while step < n_gy:
            owns[d | step] = swap(owns[d], "gy", n_gy, step)
            step <<= 1

    send_blocks(0)
    weights = (gate_weight, up_weight, down_weight)
    acts = {}

    def chunk(at, d, first_piece, count):
        if others[d] is None:
            yield
            owns[d] = pass_on(line, owns[d])
            others[d] = swap_core(parted(line, owns[d]))
            send_blocks(d)
        yield
        last, first = forward_products(
            line, core, owns[d], others[d], first_piece * piece, count * piece, piece, weights
        )
        value = first
        for step in range(n_gz - 1):
            got = hop(value, step)
            yield
            if step < n_gz - 2:
                value = add_on(line, first if step + 1 < n_gz // 2 else last, got)
        value = activations(line, last, got)
        passed = [value]
        for step in range(n_gz - 1):
            value = hop(value, step)
            yield
            value = pass_on(line, value)
            passed.append(value)
        yield
        keep, acts[at], *send = backward_products(line, core, place, passed, piece, weights)
        got = swap_core(send)
        yield
        part = add_quarters(line, keep, got, at == len(plan) - 1)
        if d:
            part = [swap(half, "gy", n_gy, d) for half in part]
            yield
            part = [pass_on(line, half) for half in part]
        parts[d].append(part)
        yield

    plan, order = plan_of(n_gy, n_gz, pieces)
    spans = []
    for d, first_piece, count in plan:
        low = (d * pieces + first_piece) * piece
        spans.append((low, low + count * piece))
    parts = [[] for _ in range(n_gy)]
    runs = [chunk(at, *entry) for at, entry in enumerate(plan)]
    for run in runs:
        next(run)
    for at in order:
        if at == WEIGHTS:
            every = [acts[i] for i in range(len(plan))]
            grads = weight_grads(
                line, core, [owns[d] for d in range(n_gy)], others, every, spans
            )
        else:
            next(runs[at])
    output, tokens_grad = final_sum(line, parts, flip, piece)
    _, gate_grad_w, up_grad_w, down_grad_w = grads
    return (output, tokens_grad, gate_grad_w, up_grad_w, down_grad_w)


def solution(mesh):
    return jax.shard_map(
        functools.partial(per_device, dict(mesh.shape)),
        mesh=mesh,
        in_specs=(
            P("gy", ("gz", "gx")),
            P("gz", ("gx", "gy")),
            P("gz", ("gx", "gy")),
            P("gz", ("gx", "gy")),
            P("gy", ("gz", "gx")),
        ),
        out_specs=(
            P("gy", ("gz", "gx")),
            P("gy", ("gz", "gx")),
            P("gz", ("gx", "gy")),
            P("gz", ("gx", "gy")),
            P("gz", ("gx", "gy")),
        ),
        check_vma=False,
    )
```
